32 devices in a mesh: groups: 2 (over x), src: 16 (over z, y, core).
Axes of the slice: x: 2, y: 2, z: 4, core: 2. Of those that a mesh axis runs over, the one named last changes fastest.
Arguments:
- source_field: float32 [32, 131072], P('groups', 'src'), parts along dimension 0, may hold values from -6 to 6
- neighbours: int32 [6, 131072], P(None, 'src'), may hold values from 0 to 8447, as said below
- slope_weights: float32 [2, 6, 131072], P(None, None, 'src'), may hold values from -2 to 2
- pair_block: int32 [16, 256], replicated, may hold values from 0 to 1023, as said below
- pair_dest: int32 [16, 256], P('src'), may hold values from 0 to 63
- remap_weights: bfloat16 [4096, 384, 128], P('src'), may hold values from -0.15625 to 0.15625
Outputs:
- remapped: float32 [32, 128, 1024], P('groups', 'src'), parts along dimension 0
- meridional: float32 [32, 128, 1024], P('groups', 'src'), parts along dimension 0
The draws below stay inside these ranges and needn't reach their ends.
There are 2 independent parts, one for each index of `groups`. The reference program is written for one: setup_inputs(seed, part) draws one part's arguments, and reference() takes and returns one part's arrays. A program takes and returns all parts, laid end to end along the dimension named above; an argument that names none is the same for every part. Nothing has to cross between parts.
Inputs may be any that keep to these rules, and one draw needn't show every extreme that they name: `neighbours`: entry (k, c) is a position in cell c's partition of 8192 cells extended by the last 128 cells of the previous partition before and the first 128 of the next after, the partitions closing into a loop; it lies within 128 of cell c's own position. `pair_block`: an entry names source block (partition * 64 + block of that partition). In every row at most 16 entries name blocks of one partition, and they name at most 8 distinct blocks.
All inputs are finite; a program needn't handle non-finite values.
Results may differ from the reference program's by a relative error of at most 0.0029.
Values may be sent and summed in bfloat16 or wider, within the bound.
No kernel may reach another device: no remote copies, remote signals or barrier semaphores. Data moves between devices by JAX's collectives and lax.ppermute only.
A program may use at most 128 MiB of HBM per device.

```python
import jax
import jax.numpy as jnp
from jax import lax

L = 16
K = 6
BLK = 128
HALO = 128
NB = 64
LAT_DEV = 8
LONB = 8
PER_BLOCK = 4
TILES = 16
SRC_DEV = 8192
CELLS = 131072
DB = 64
PMAX = 256
CAP = 16
DCAP = 8
LAT = 128
LON = 1024
LOAD_LO = 16


def draw_neighbours(key, part):
    key = jax.random.fold_in(key, 12)
    offsets = jax.random.randint(key, (K, CELLS), -HALO, HALO + 1)
    position = jnp.arange(CELLS, dtype=jnp.int32) % SRC_DEV
    first_row = jnp.where(position == 0, -HALO, jnp.where(position == SRC_DEV - 1, HALO, offsets[0]))
    offsets = offsets.at[0].set(first_row)
    return (HALO + position[None, :] + offsets).astype(jnp.int32)


def draw_pair_block(key, part):
    key = jax.random.fold_in(key, 11)
    key_count, key_order, key_base, key_step, key_mix = jax.random.split(key, 5)
    counts = jax.random.randint(key_count, (TILES, TILES), LOAD_LO, CAP + 1)
    counts = counts.at[:, 0].set(CAP).at[:, 1].set(LOAD_LO).at[:, 2].set(LOAD_LO)
    ends = jnp.cumsum(counts, axis=1)
    starts = ends - counts
    slot_ids = jnp.arange(PMAX, dtype=jnp.int32)
    group = jnp.sum((ends[:, None, :] <= slot_ids[None, :, None]).astype(jnp.int32), axis=2)
    within = slot_ids[None, :] - jnp.take_along_axis(starts, group, axis=1)
    rest = jax.vmap(lambda sub: jax.random.permutation(sub, TILES - 3))(jax.random.split(key_order, TILES))
    rest = 1 + rest.astype(jnp.int32)
    rest = jnp.where(rest >= TILES // 2, rest + 1, rest)
    lead = jnp.broadcast_to(jnp.array([0, TILES - 1, TILES // 2], dtype=jnp.int32)[None, :], (TILES, 3))
    shifts = jnp.concatenate([lead, rest], axis=1)
    row_ids = jnp.arange(TILES, dtype=jnp.int32)
    order = (row_ids[:, None] + shifts) % TILES
    base = jax.random.randint(key_base, (TILES, TILES), 0, NB)
    base = base.at[:, 0].set(0).at[:, 1].set(NB - 1)
    stride = 1 + 2 * jax.random.randint(key_step, (TILES, TILES), 0, NB)
    source = jnp.take_along_axis(order, group, axis=1)
    unique_rank = within * DCAP // CAP
    block = (jnp.take_along_axis(base, group, axis=1) + unique_rank * jnp.take_along_axis(stride, group, axis=1)) % NB
    named = source * NB + block
    shuffles = jax.vmap(lambda sub: jax.random.permutation(sub, PMAX))(jax.random.split(key_mix, TILES))
    return jnp.take_along_axis(named, shuffles, axis=1).astype(jnp.int32)


def with_ends(drawn, own_key, smallest, largest):
    longest = drawn.shape.index(max(drawn.shape))
    spots = []
    for shift in (0, 1):
        where = [jax.random.randint(jax.random.fold_in(own_key, axis), (), 0, length) for axis, length in enumerate(drawn.shape)]
        where[longest] = (where[longest] + shift) % drawn.shape[longest]
        spots.append(tuple(where))
    return drawn.at[spots[0]].set(smallest).at[spots[1]].set(largest)


def steps_of(rng, shape, cuts, smallest, high):
    gain, own = 1.0, jax.random.fold_in(rng, 6)
    for dim, parts in cuts:
        heights = jnp.exp(jax.random.uniform(jax.random.fold_in(own, dim), (parts,), jnp.float32, smallest / len(cuts), high / len(cuts)))
        gain = gain * jnp.repeat(heights, shape[dim] // parts).reshape([-1 if axis == dim else 1 for axis in range(len(shape))])
    return gain


def centred(rng, extent, spread, bound, shards=(), kind=jnp.bfloat16):
    entries = spread * jax.random.normal(rng, extent, jnp.float32)
    if shards:
        entries = entries * steps_of(rng, extent, shards, -0.22, 0.18)
    return jnp.clip(entries, -bound, bound).astype(kind)


def setup_inputs(seed: int = 0, part: int = 0) -> dict:
    seeds = jax.random.split(jax.random.key(seed), 7)
    own_keys = jax.random.split(jax.random.fold_in(seeds[6], part), 7)
    source_field = centred(own_keys[0], (L, CELLS), 1.0, 6.0, ((1, 16),), jnp.float32)
    neighbours = draw_neighbours(jax.random.fold_in(seeds[6], 71), part)
    slope_weights = centred(seeds[2], (2, K, CELLS), 0.3, 2.0, ((2, 16),), jnp.float32)
    pair_block = draw_pair_block(jax.random.fold_in(seeds[6], 71), part)
    pair_dest = with_ends(jax.random.randint(seeds[4], (TILES, PMAX), 0, DB), jax.random.fold_in(seeds[4], 1), 0, DB - 1).astype(jnp.int32)
    remap_weights = centred(seeds[5], (TILES * PMAX, 3 * BLK, BLK), (3 * BLK * PER_BLOCK) ** -0.5, 0.15625, ((0, 16),))
    return dict(source_field=source_field, neighbours=neighbours, slope_weights=slope_weights, pair_block=pair_block, pair_dest=pair_dest, remap_weights=remap_weights)


def reference(source_field, neighbours, slope_weights, pair_block, pair_dest, remap_weights):
    cell_count = source_field.shape[1]
    owner = jnp.arange(cell_count, dtype=jnp.int32) // SRC_DEV
    global_nbr = (neighbours + (owner * SRC_DEV - HALO)[None, :]) % cell_count
    slope_east = jnp.zeros(source_field.shape, jnp.float32)
    slope_north = jnp.zeros(source_field.shape, jnp.float32)
    for offset in range(K):
        difference = jnp.take(source_field, global_nbr[offset], axis=1) - source_field
        slope_east = slope_east + slope_weights[0, offset][None, :] * difference
        slope_north = slope_north + slope_weights[1, offset][None, :] * difference
    stacked = jnp.stack([source_field, slope_east, slope_north])
    stacked = stacked.reshape(3, L, TILES * NB, BLK).transpose(2, 1, 0, 3)
    moments = stacked.reshape(TILES * NB, L, 3 * BLK).astype(jnp.bfloat16)
    weight_rows = remap_weights.reshape(TILES, PMAX, 3 * BLK, BLK)

    def one_tile(inputs):
        block_row, dest_row, weight_tile = inputs
        chosen = jnp.take(moments, block_row, axis=0).astype(jnp.float32)
        contrib = jnp.einsum("pli,pio->plo", chosen, weight_tile.astype(jnp.float32))
        one_hot = (dest_row[None, :] == jnp.arange(DB, dtype=jnp.int32)[:, None]).astype(jnp.float32)
        tile_sum = jnp.dot(one_hot, contrib.reshape(PMAX, L * BLK), precision=lax.Precision.HIGHEST)
        return tile_sum.reshape(DB, L, BLK)

    all_tiles = lax.map(one_tile, (pair_block, pair_dest, weight_rows))
    remapped = all_tiles.reshape(TILES, LAT_DEV, LONB, L, BLK).transpose(3, 0, 1, 2, 4).reshape(L, LAT, LON)
    padded = jnp.pad(remapped, ((0, 0), (1, 1), (0, 0)))
    meridional = 0.5 * (padded[:, 2:] - padded[:, :-2])
    return remapped, meridional
```

```python
import functools

import jax
import jax.numpy as jnp
from jax import lax
from jax.experimental import pallas as pl
from jax.experimental.pallas import tpu as pltpu
from jax.sharding import PartitionSpec as P

K = 6
BLK = 128
HALO = 128
NB = 64
LAT_DEV = 8
LONB = 8
DB = 64
ROWS = 9
CODE = 32767.0
FIELD_BOUND = 6.0
WEIGHT_BOUND = 2.0
VMEM = pl.BlockSpec(memory_space=pltpu.VMEM)
SMEM = pl.BlockSpec(memory_space=pltpu.SMEM)
ANY = pl.BlockSpec(memory_space=pl.ANY)


def encode(values, bound):
    scaled = jnp.abs(values) * (1.0 / bound)
    root = jnp.exp2(jnp.log2(jnp.maximum(scaled, 1e-30)) * 0.2)
    code = jnp.minimum(jnp.floor(root * CODE + 0.5), CODE)
    code = jnp.where(scaled > 1e-24, code, 0.0)
    return jnp.where(values < 0, -code, code).astype(jnp.int32)


def pack(high, low):
    return high * 65536 + (low + 32768)


def unpack(word):
    return word >> 16, (word & 65535) - 32768


def decode(code, bound):
    real = code.astype(jnp.float32)
    square = real * real
    return square * square * (real * (bound / CODE**5))


def pack_field_kernel(field_ref, out_ref):
    half = field_ref.shape[0] // 2
    high = encode(field_ref[:half], FIELD_BOUND)
    low = encode(field_ref[half:], FIELD_BOUND)
    out_ref[...] = pack(high, low)


def pack_field(field):
    levels, cells = field.shape
    step = 2048
    return pl.pallas_call(
        pack_field_kernel,
        grid=(cells // step,),
        in_specs=[pl.BlockSpec((levels, step), lambda i: (0, i))],
        out_specs=pl.BlockSpec((levels // 2, step), lambda i: (0, i)),
        out_shape=jax.ShapeDtypeStruct((levels // 2, cells), jnp.int32),
    )(field)


def pack_geometry_kernel(neighbours_ref, weights_ref, out_ref):
    step = out_ref.shape[1]
    column = lax.broadcasted_iota(jnp.int32, (1, step), 1) + pl.program_id(0) * step
    start = (column >> 7) << 7
    relative = neighbours_ref[...] - start
    for k in range(K):
        east = encode(weights_ref[k, 0:1, :], WEIGHT_BOUND)
        north = encode(weights_ref[k, 1:2, :], WEIGHT_BOUND)
        out_ref[k : k + 1, :] = pack(east, north)
    for k in range(K // 2):
        out_ref[K + k : K + k + 1, :] = pack(relative[k : k + 1], relative[k + 3 : k + 4])


def pack_geometry(neighbours, slope_weights):
    cells = neighbours.shape[1]
    step = 2048
    return pl.pallas_call(
        pack_geometry_kernel,
        grid=(cells // step,),
        in_specs=[
            pl.BlockSpec((K, step), lambda i: (0, i)),
            pl.BlockSpec((K, 2, step), lambda i: (0, 0, i)),
        ],
        out_specs=pl.BlockSpec((16, step), lambda i: (0, i)),
        out_shape=jax.ShapeDtypeStruct((16, cells), jnp.int32),
    )(neighbours, jnp.transpose(slope_weights, (1, 0, 2)))


def choose_geometry_kernel(block_ref, packed_ref, out_ref):
    tiles, slots = block_ref.shape

    def tile(t, carry):
        for s in range(slots):
            lanes = pl.ds(pl.multiple_of(block_ref[t, s] * BLK, BLK), BLK)
            out_ref[t, s * ROWS : (s + 1) * ROWS, :] = packed_ref[:ROWS, lanes]
        return carry

    lax.fori_loop(0, tiles, tile, 0)


def choose_geometry(blocks, packed):
    tiles, slots = blocks.shape
    return pl.pallas_call(
        choose_geometry_kernel,
        in_specs=[SMEM, VMEM],
        out_specs=VMEM,
        out_shape=jax.ShapeDtypeStruct((tiles, slots * ROWS, BLK), jnp.int32),
    )(blocks, packed)


def ranks(present):
    ids = jnp.arange(NB, dtype=jnp.int32)
    before = (ids[:, None] < ids[None, :])[None]
    return jnp.sum((present[:, :, None] & before).astype(jnp.int32), axis=1)


def blocks_of_slots(present, rank, slots):
    ids = jnp.arange(NB, dtype=jnp.int32)
    wanted = jnp.arange(slots, dtype=jnp.int32)
    match = present[:, :, None] & (rank[:, :, None] == wanted[None, None, :])
    return jnp.sum(jnp.where(match, ids[None, :, None], 0), axis=1)


def slopes_and_moments(window, words):
    low_block, mid_block, high_block = window
    east_code, north_code = unpack(words[0:K])
    east_weight = decode(east_code, WEIGHT_BOUND)
    north_weight = decode(north_code, WEIGHT_BOUND)
    first, second = unpack(words[K : K + 3])
    own = [decode(code, FIELD_BOUND) for code in unpack(mid_block)]
    east = [jnp.zeros_like(own[0]) for _ in own]
    north = [jnp.zeros_like(own[0]) for _ in own]
    shape = mid_block.shape
    for k in range(K):
        row = first[k : k + 1] if k < 3 else second[k - 3 : k - 2]
        place = jnp.broadcast_to(row, shape)
        lane = place & (BLK - 1)
        picked = [
            jnp.take_along_axis(part, lane, axis=1, mode="promise_in_bounds")
            for part in (low_block, mid_block, high_block)
        ]
        word = jnp.where(place < BLK, picked[0], jnp.where(place < 2 * BLK, picked[1], picked[2]))
        for side, code in enumerate(unpack(word)):
            difference = decode(code, FIELD_BOUND) - own[side]
            east[side] = east[side] + east_weight[k : k + 1] * difference
            north[side] = north[side] + north_weight[k : k + 1] * difference
    return [jnp.concatenate(part, axis=0).astype(jnp.bfloat16) for part in (own, east, north)]


def remap_kernel(parts, chunk, slots, *refs):
    me_ref, block_ref, slot_ref, dest_ref, geometry_ref, weights_ref = refs[:6]
    shards = refs[6 : 6 + len(parts)]
    out_ref, edge_ref = refs[6 + len(parts) : 8 + len(parts)]
    field, moments, weights, total, field_sem, weight_sem = refs[8 + len(parts) :]
    partitions = block_ref.shape[0]
    cells = NB * BLK
    blocks = partitions * NB
    pairs = slot_ref.shape[0]
    chunks = pairs // chunk
    me = me_ref[0]

    copies = []
    for (code, start, size), shard in zip(parts, shards):
        if code is None:
            target = field
        else:
            lanes = pl.ds(pl.multiple_of((me ^ code) * cells + start, BLK), size)
            target = field.at[:, lanes]
        copies.append(pltpu.make_async_copy(shard, target, field_sem))
    for copy in copies:
        copy.start()

    def weight_copy(c):
        piece = pl.ds(c * chunk, chunk)
        return pltpu.make_async_copy(weights_ref.at[piece], weights.at[piece], weight_sem.at[c])

    for c in range(chunks):
        weight_copy(c).start()
    total[...] = jnp.zeros_like(total)
    for copy in copies:
        copy.wait()

    def source(q, carry):
        for s in range(slots):
            block = q * NB + block_ref[q, s]
            window = []
            for shift in (-1, 0, 1):
                near = lax.rem(block + (shift + blocks), blocks)
                window.append(field[:, pl.ds(pl.multiple_of(near * BLK, BLK), BLK)])
            words = geometry_ref[q, s * ROWS : (s + 1) * ROWS, :]
            for m, part in enumerate(slopes_and_moments(window, words)):
                moments[q * slots + s, :, m * BLK : (m + 1) * BLK] = part
        return carry

    lax.fori_loop(0, partitions, source, 0)

    def piece(c, carry):
        weight_copy(c).wait()
        for i in range(chunk):
            p = c * chunk + i
            product = jnp.dot(moments[slot_ref[p]], weights[p], preferred_element_type=jnp.float32)
            dest = dest_ref[p]
            rows = pl.ds(dest >> 3, 16, stride=LAT_DEV)
            total[dest & 7, rows, :] = total[dest & 7, rows, :] + product
        return carry

    lax.fori_loop(0, chunks, piece, 0)
    levels = out_ref.shape[0]
    for o in range(LONB):
        lanes = slice(o * BLK, (o + 1) * BLK)
        out_ref[:, :, lanes] = total[o].reshape(levels, LAT_DEV, BLK)
        edge_ref[0, :, lanes] = total[o, pl.ds(0, levels, stride=LAT_DEV), :]
        edge_ref[1, :, lanes] = total[o, pl.ds(LAT_DEV - 1, levels, stride=LAT_DEV), :]


def remap(me, blocks, slot, dest, geometry, weights, parts, shards, levels):
    partitions, slots = blocks.shape
    pairs = slot.shape[0]
    chunk = 16
    return pl.pallas_call(
        functools.partial(remap_kernel, parts, chunk, slots),
        in_specs=[SMEM] * 4 + [VMEM, ANY] + [ANY] * len(shards),
        out_specs=(VMEM, VMEM),
        out_shape=(
            jax.ShapeDtypeStruct((levels, LAT_DEV, LONB * BLK), jnp.float32),
            jax.ShapeDtypeStruct((2, levels, LONB * BLK), jnp.float32),
        ),
        scratch_shapes=[
            pltpu.VMEM((levels // 2, partitions * NB * BLK), jnp.int32),
            pltpu.VMEM((partitions * slots, levels, 3 * BLK), jnp.bfloat16),
            pltpu.VMEM(weights.shape, jnp.bfloat16),
            pltpu.VMEM((LONB, levels * LAT_DEV, BLK), jnp.float32),
            pltpu.SemaphoreType.DMA,
            pltpu.SemaphoreType.DMA((pairs // chunk,)),
        ],
        compiler_params=pltpu.CompilerParams(vmem_limit_bytes=56 * 1024 * 1024),
    )(me, blocks, slot, dest, geometry, weights, *shards)


def share_field(packed, count):
    if count != 16:
        whole = lax.all_gather(packed, "src", axis=1, tiled=True)
        return [(None, 0, whole.shape[1])], [whole]

    def swap(array, code):
        return lax.ppermute(array, "src", [(i, i ^ code) for i in range(count)])

    cells = packed.shape[1]
    half = cells // 2
    far = swap(packed, 8)
    z = swap(packed, 4)
    y = swap(packed, 2)
    diagonal = swap(z, 2)
    far_z = swap(far, 4)
    far_y = swap(far, 2)
    far_low = swap(far_z[:, :half], 2)
    far_high = swap(far_y[:, half:], 4)
    held = [
        (0, 0, packed),
        (2, 0, y),
        (4, 0, z),
        (6, 0, diagonal),
        (8, 0, far),
        (12, 0, far_z),
        (10, 0, far_y),
        (14, 0, far_low),
        (14, half, far_high),
    ]
    held = held + [(code ^ 1, start, swap(array, 1)) for code, start, array in held]
    parts = [(code, start, array.shape[1]) for code, start, array in held]
    return parts, [array for _, _, array in held]


def local(source_field, neighbours, slope_weights, pair_block, pair_dest, remap_weights):
    levels, cell_count = source_field.shape
    own_index = lax.axis_index("src")
    partitions = lax.axis_size("src")
    pair_total = pair_block.shape[1]
    slots = max(1, pair_total // partitions // 2)
    ids = jnp.arange(NB, dtype=jnp.int32)

    packed = pack_field(source_field)
    parts, shards = share_field(packed, partitions)

    own_names = own_index * NB + ids
    asked = jnp.any(pair_block[:, :, None] == own_names[None, None, :], axis=1)
    outgoing_blocks = blocks_of_slots(asked, ranks(asked), slots)
    geometry = choose_geometry(outgoing_blocks, pack_geometry(neighbours, slope_weights))
    geometry = lax.all_to_all(geometry, "src", split_axis=0, concat_axis=0, tiled=True)

    row = lax.dynamic_index_in_dim(pair_block, own_index, 0, keepdims=False)
    names = jnp.arange(partitions * NB, dtype=jnp.int32)
    same = row[:, None] == names[None, :]
    needed = jnp.any(same, axis=0).reshape(partitions, NB)
    rank = ranks(needed)
    blocks = blocks_of_slots(needed, rank, slots)
    slot_of_name = (jnp.arange(partitions, dtype=jnp.int32)[:, None] * slots + rank).reshape(-1)
    slot = jnp.sum(jnp.where(same, slot_of_name[None, :], 0), axis=1)

    remapped, edges = remap(
        own_index.reshape(1), blocks, slot, pair_dest[0], geometry, remap_weights, parts, shards, levels
    )
    up = [(i, i + 1) for i in range(partitions - 1)]
    down = [(i + 1, i) for i in range(partitions - 1)]
    below = lax.ppermute(edges[1], "src", up)
    above = lax.ppermute(edges[0], "src", down)
    padded = jnp.concatenate([below[:, None], remapped, above[:, None]], axis=1)
    meridional = 0.5 * (padded[:, 2:] - padded[:, :-2])
    return remapped, meridional


def solution(mesh):
    return jax.shard_map(
        local,
        mesh=mesh,
        in_specs=(
            P("groups", "src"),
            P(None, "src"),
            P(None, None, "src"),
            P(),
            P("src", None),
            P("src", None, None),
        ),
        out_specs=(P("groups", "src", None), P("groups", "src", None)),
        check_vma=False,
    )
```

```python
import functools

import jax
import jax.numpy as jnp
from jax import lax
from jax.experimental import pallas as pl
from jax.experimental.pallas import tpu as pltpu
from jax.sharding import PartitionSpec as P

K = 6
BLK = 128
HALO = 128
NB = 64
LAT_DEV = 8
LONB = 8
DB = 64
ROWS = 9
CODE = 32767.0
FIELD_BOUND = 6.0
WEIGHT_BOUND = 2.0
VMEM = pl.BlockSpec(memory_space=pltpu.VMEM)
SMEM = pl.BlockSpec(memory_space=pltpu.SMEM)
ANY = pl.BlockSpec(memory_space=pl.ANY)


def encode(values, bound):
    scaled = jnp.abs(values) * (1.0 / bound)
    root = jnp.exp2(jnp.log2(jnp.maximum(scaled, 1e-30)) * 0.2)
    code = jnp.minimum(jnp.floor(root * CODE + 0.5), CODE)
    code = jnp.where(scaled > 1e-24, code, 0.0)
    return jnp.where(values < 0, -code, code).astype(jnp.int32)


def pack(high, low):
    return high * 65536 + (low + 32768)


def unpack(word):
    return word >> 16, (word & 65535) - 32768


def decode(code, bound):
    real = code.astype(jnp.float32)
    square = real * real
    return square * square * (real * (bound / CODE**5))


def prepare_kernel(block_ref, field_ref, neighbours_ref, weights_ref, field_out, geometry_out, packed):
    tiles, slots = block_ref.shape
    half = field_ref.shape[0] // 2
    cells = neighbours_ref.shape[1]
    step = 1024

    def piece(i, carry):
        lanes = pl.ds(pl.multiple_of(i * step, step), step)
        high = encode(field_ref[:half, lanes], FIELD_BOUND)
        low = encode(field_ref[half:, lanes], FIELD_BOUND)
        field_out[:, lanes] = pack(high, low)
        column = lax.broadcasted_iota(jnp.int32, (1, step), 1) + i * step
        start = (column >> 7) << 7
        relative = neighbours_ref[:, lanes] - start
        east = encode(weights_ref[:, 0, lanes], WEIGHT_BOUND)
        north = encode(weights_ref[:, 1, lanes], WEIGHT_BOUND)
        packed[:K, lanes] = pack(east, north)
        packed[K:ROWS, lanes] = pack(relative[: K // 2], relative[K // 2 :])
        return carry

    lax.fori_loop(0, cells // step, piece, 0)

    def tile(t, carry):
        for s in range(slots):
            lanes = pl.ds(pl.multiple_of(block_ref[t, s] * BLK, BLK), BLK)
            geometry_out[t, s * ROWS : (s + 1) * ROWS, :] = packed[:ROWS, lanes]
        return carry

    lax.fori_loop(0, tiles, tile, 0)


def prepare(blocks, field, neighbours, slope_weights):
    tiles, slots = blocks.shape
    levels, cells = field.shape
    return pl.pallas_call(
        prepare_kernel,
        in_specs=[SMEM, VMEM, VMEM, VMEM],
        out_specs=(VMEM, VMEM),
        out_shape=(
            jax.ShapeDtypeStruct((levels // 2, cells), jnp.int32),
            jax.ShapeDtypeStruct((tiles, slots * ROWS, BLK), jnp.int32),
        ),
        scratch_shapes=[pltpu.VMEM((16, cells), jnp.int32)],
    )(blocks, field, neighbours, jnp.transpose(slope_weights, (1, 0, 2)))


def ranks(present):
    ids = jnp.arange(NB, dtype=jnp.int32)
    before = (ids[:, None] < ids[None, :])[None]
    return jnp.sum((present[:, :, None] & before).astype(jnp.int32), axis=1)


def blocks_of_slots(present, rank, slots):
    ids = jnp.arange(NB, dtype=jnp.int32)
    wanted = jnp.arange(slots, dtype=jnp.int32)
    match = present[:, :, None] & (rank[:, :, None] == wanted[None, None, :])
    return jnp.sum(jnp.where(match, ids[None, :, None], 0), axis=1)


def slopes_and_moments(window, words):
    low_block, mid_block, high_block = window
    east_code, north_code = unpack(words[0:K])
    east_weight = decode(east_code, WEIGHT_BOUND)
    north_weight = decode(north_code, WEIGHT_BOUND)
    first, second = unpack(words[K : K + 3])
    own = [decode(code, FIELD_BOUND) for code in unpack(mid_block)]
    east = [jnp.zeros_like(own[0]) for _ in own]
    north = [jnp.zeros_like(own[0]) for _ in own]
    shape = mid_block.shape
    for k in range(K):
        row = first[k : k + 1] if k < 3 else second[k - 3 : k - 2]
        place = jnp.broadcast_to(row, shape)
        lane = place & (BLK - 1)
        picked = [
            jnp.take_along_axis(part, lane, axis=1, mode="promise_in_bounds")
            for part in (low_block, mid_block, high_block)
        ]
        word = jnp.where(place < BLK, picked[0], jnp.where(place < 2 * BLK, picked[1], picked[2]))
        for side, code in enumerate(unpack(word)):
            difference = decode(code, FIELD_BOUND) - own[side]
            east[side] = east[side] + east_weight[k : k + 1] * difference
            north[side] = north[side] + north_weight[k : k + 1] * difference
    return [jnp.concatenate(part, axis=0).astype(jnp.bfloat16) for part in (own, east, north)]


def remap_kernel(parts, chunk, slots, shares, *refs):
    me_ref, block_ref, slot_ref, dest_ref = refs[:4]
    geometry_refs = refs[4 : 4 + shares]
    refs = refs[4 + shares :]
    weights_ref, refs = refs[0], refs[1:]
    shards = refs[: len(parts)]
    out_ref, top_ref, bottom_ref = refs[len(parts) : 3 + len(parts)]
    field, moments, weights, total, field_sem, weight_sem = refs[3 + len(parts) :]
    partitions = block_ref.shape[0]
    cells = NB * BLK
    blocks = partitions * NB
    pairs = slot_ref.shape[0]
    chunks = pairs // chunk
    me = me_ref[0]
    share = slots // shares

    copies = []
    for (code, start, size), shard in zip(parts, shards):
        if code is None:
            target = field
        else:
            lanes = pl.ds(pl.multiple_of((me ^ code) * cells + start, BLK), size)
            target = field.at[:, lanes]
        copies.append(pltpu.make_async_copy(shard, target, field_sem))
    for copy in copies:
        copy.start()

    def weight_copy(c):
        piece = pl.ds(c * chunk, chunk)
        return pltpu.make_async_copy(weights_ref.at[piece], weights.at[piece], weight_sem.at[c])

    for c in range(chunks):
        weight_copy(c).start(priority=1)
    total[...] = jnp.zeros_like(total)
    for copy in copies:
        copy.wait()

    def source(q, carry):
        for j in range(slots):
            part = j // share
            s = (part ^ me_ref[1]) * share + j % share
            block = q * NB + block_ref[q, s]
            window = []
            for shift in (-1, 0, 1):
                near = lax.rem(block + (shift + blocks), blocks)
                window.append(field[:, pl.ds(pl.multiple_of(near * BLK, BLK), BLK)])
            row = j % share * ROWS
            words = geometry_refs[part][q, row : row + ROWS, :]
            for m, moment in enumerate(slopes_and_moments(window, words)):
                moments[q * slots + s, :, m * BLK : (m + 1) * BLK] = moment
        return carry

    lax.fori_loop(0, partitions, source, 0)

    def piece(c, carry):
        weight_copy(c).wait()
        for i in range(chunk):
            p = c * chunk + i
            product = jnp.dot(moments[slot_ref[p]], weights[p], preferred_element_type=jnp.float32)
            dest = dest_ref[p]
            rows = pl.ds(dest >> 3, 16, stride=LAT_DEV)
            total[dest & 7, rows, :] = total[dest & 7, rows, :] + product
        return carry

    lax.fori_loop(0, chunks, piece, 0)
    levels = out_ref.shape[0]
    for o in range(LONB):
        lanes = slice(o * BLK, (o + 1) * BLK)
        out_ref[:, :, lanes] = total[o].reshape(levels, LAT_DEV, BLK)
        top_ref[:, lanes] = total[o, pl.ds(0, levels, stride=LAT_DEV), :]
        bottom_ref[:, lanes] = total[o, pl.ds(LAT_DEV - 1, levels, stride=LAT_DEV), :]


def remap(me, blocks, slot, dest, geometry, weights, parts, shards, levels):
    partitions, slots = blocks.shape
    pairs = slot.shape[0]
    chunk = 16
    return pl.pallas_call(
        functools.partial(remap_kernel, parts, chunk, slots, len(geometry)),
        in_specs=[SMEM] * 4 + [VMEM] * len(geometry) + [ANY] + [ANY] * len(shards),
        out_specs=(VMEM, VMEM, VMEM),
        out_shape=(
            jax.ShapeDtypeStruct((levels, LAT_DEV, LONB * BLK), jnp.float32),
            jax.ShapeDtypeStruct((levels, LONB * BLK), jnp.float32),
            jax.ShapeDtypeStruct((levels, LONB * BLK), jnp.float32),
        ),
        scratch_shapes=[
            pltpu.VMEM((levels // 2, partitions * NB * BLK), jnp.int32),
            pltpu.VMEM((partitions * slots, levels, 3 * BLK), jnp.bfloat16),
            pltpu.VMEM(weights.shape, jnp.bfloat16),
            pltpu.VMEM((LONB, levels * LAT_DEV, BLK), jnp.float32),
            pltpu.SemaphoreType.DMA,
            pltpu.SemaphoreType.DMA((pairs // chunk,)),
        ],
        compiler_params=pltpu.CompilerParams(vmem_limit_bytes=56 * 1024 * 1024),
    )(me, blocks, slot, dest, *geometry, weights, *shards)


def share_field(packed, count, beside):
    if count != 16:
        whole = lax.all_gather(packed, "src", axis=1, tiled=True)
        return [(None, 0, whole.shape[1])], [whole], beside

    def swap(array, code):
        return lax.ppermute(array, "src", [(i, i ^ code) for i in range(count)])

    far = swap(packed, 8)
    z = swap(packed, 4)
    y = swap(packed, 2)
    far, z, y = lax.optimization_barrier((far, z, y))
    far_z = swap(far, 4)
    far_y = swap(far, 2)
    diagonal = swap(z, 2)
    far_z, far_y, beside = lax.optimization_barrier((far_z, far_y, beside))
    far_diagonal = swap(far_z, 2)
    held = [
        (0, 0, packed),
        (2, 0, y),
        (4, 0, z),
        (6, 0, diagonal),
        (8, 0, far),
        (12, 0, far_z),
        (10, 0, far_y),
        (14, 0, far_diagonal),
    ]
    held = held + [(code ^ 1, start, swap(array, 1)) for code, start, array in held]
    parts = [(code, start, array.shape[1]) for code, start, array in held]
    return parts, [array for _, _, array in held], beside


def local(source_field, neighbours, slope_weights, pair_block, pair_dest, remap_weights):
    levels, cell_count = source_field.shape
    own_index = lax.axis_index("src")
    partitions = lax.axis_size("src")
    pair_total = pair_block.shape[1]
    slots = max(1, pair_total // partitions // 2)
    ids = jnp.arange(NB, dtype=jnp.int32)

    own_names = own_index * NB + ids
    group = lax.axis_index("groups")
    shares = lax.axis_size("groups") if lax.axis_size("groups") == 2 else 1
    asked = jnp.any(pair_block[:, :, None] == own_names[None, None, :], axis=1)
    outgoing_blocks = blocks_of_slots(asked, ranks(asked), slots)
    share = slots // shares
    if shares == 2:
        outgoing_blocks = lax.dynamic_slice_in_dim(outgoing_blocks, group * share, share, 1)
    packed, geometry = prepare(outgoing_blocks, source_field, neighbours, slope_weights)
    geometry = [lax.all_to_all(geometry, "src", split_axis=0, concat_axis=0, tiled=True)]
    first = jnp.zeros((), jnp.int32)
    if shares == 2:
        geometry.append(lax.ppermute(geometry[0], "groups", [(0, 1), (1, 0)]))
        first = group

    row = lax.dynamic_index_in_dim(pair_block, own_index, 0, keepdims=False)
    names = jnp.arange(partitions * NB, dtype=jnp.int32)
    same = row[:, None] == names[None, :]
    needed = jnp.any(same, axis=0).reshape(partitions, NB)
    rank = ranks(needed)
    blocks = blocks_of_slots(needed, rank, slots)
    slot_of_name = (jnp.arange(partitions, dtype=jnp.int32)[:, None] * slots + rank).reshape(-1)
    slot = jnp.sum(jnp.where(same, slot_of_name[None, :], 0), axis=1)

    parts, shards, (slot, blocks) = share_field(packed, partitions, (slot, blocks))
    remapped, top, bottom = remap(
        jnp.stack([own_index, first]), blocks, slot, pair_dest[0], geometry, remap_weights, parts, shards, levels
    )
    up = [(i, i + 1) for i in range(partitions - 1)]
    down = [(i + 1, i) for i in range(partitions - 1)]
    below = lax.ppermute(bottom, "src", up)
    above = lax.ppermute(top, "src", down)
    padded = jnp.concatenate([below[:, None], remapped, above[:, None]], axis=1)
    meridional = 0.5 * (padded[:, 2:] - padded[:, :-2])
    return remapped, meridional


def solution(mesh):
    return jax.shard_map(
        local,
        mesh=mesh,
        in_specs=(
            P("groups", "src"),
            P(None, "src"),
            P(None, None, "src"),
            P(),
            P("src", None),
            P("src", None, None),
        ),
        out_specs=(P("groups", "src", None), P("groups", "src", None)),
        check_vma=False,
    )
```

```python
import functools

import jax
import jax.numpy as jnp
from jax import lax
from jax.experimental import pallas as pl
from jax.experimental.pallas import tpu as pltpu
from jax.sharding import PartitionSpec as P

K = 6
BLK = 128
HALO = 128
NB = 64
LAT_DEV = 8
LONB = 8
CELLS = NB * BLK
ROWS = 9
CODE = 32767.0
FIELD_BOUND = 6.0
WEIGHT_BOUND = 2.0
VMEM = pl.BlockSpec(memory_space=pltpu.VMEM)
SMEM = pl.BlockSpec(memory_space=pltpu.SMEM)
ANY = pl.BlockSpec(memory_space=pl.ANY)


def encode(values, bound):
    scaled = jnp.abs(values) * (1.0 / bound)
    root = jnp.exp2(jnp.log2(jnp.maximum(scaled, 1e-30)) * 0.2)
    code = jnp.minimum(jnp.floor(root * CODE + 0.5), CODE)
    code = jnp.where(scaled > 1e-24, code, 0.0)
    return jnp.where(values < 0, -code, code).astype(jnp.int32)


def pack(high, low):
    return high * 65536 + (low + 32768)


def unpack(word):
    return word >> 16, (word & 65535) - 32768


def decode(code, bound):
    real = code.astype(jnp.float32)
    square = real * real
    return square * square * (real * (bound / CODE**5))


def pack_field_kernel(field_ref, out_ref):
    half = field_ref.shape[0] // 2
    step = 1024

    def piece(i, carry):
        lanes = pl.ds(pl.multiple_of(i * step, step), step)
        high = encode(field_ref[:half, lanes], FIELD_BOUND)
        low = encode(field_ref[half:, lanes], FIELD_BOUND)
        out_ref[:, lanes] = pack(high, low)
        return carry

    lax.fori_loop(0, field_ref.shape[1] // step, piece, 0)


def pack_field(field):
    levels, cells = field.shape
    return pl.pallas_call(
        pack_field_kernel,
        in_specs=[VMEM],
        out_specs=VMEM,
        out_shape=jax.ShapeDtypeStruct((levels // 2, cells), jnp.int32),
    )(field)


def geometry_kernel(block_ref, neighbours_ref, weights_ref, out_ref, packed):
    tiles, slots = block_ref.shape
    cells = neighbours_ref.shape[1]
    step = 1024

    def piece(i, carry):
        lanes = pl.ds(pl.multiple_of(i * step, step), step)
        column = lax.broadcasted_iota(jnp.int32, (1, step), 1) + i * step
        start = (column >> 7) << 7
        relative = neighbours_ref[:, lanes] - start
        east = encode(weights_ref[:, 0, lanes], WEIGHT_BOUND)
        north = encode(weights_ref[:, 1, lanes], WEIGHT_BOUND)
        packed[:K, lanes] = pack(east, north)
        packed[K:ROWS, lanes] = pack(relative[: K // 2], relative[K // 2 :])
        return carry

    lax.fori_loop(0, cells // step, piece, 0)

    def tile(t, carry):
        for s in range(slots):
            lanes = pl.ds(pl.multiple_of(block_ref[t, s] * BLK, BLK), BLK)
            out_ref[t, s * ROWS : (s + 1) * ROWS, :] = packed[:ROWS, lanes]
        return carry

    lax.fori_loop(0, tiles, tile, 0)


def choose_geometry(blocks, neighbours, slope_weights):
    tiles, slots = blocks.shape
    return pl.pallas_call(
        geometry_kernel,
        in_specs=[SMEM, VMEM, VMEM],
        out_specs=VMEM,
        out_shape=jax.ShapeDtypeStruct((tiles, slots * ROWS, BLK), jnp.int32),
        scratch_shapes=[pltpu.VMEM((16, neighbours.shape[1]), jnp.int32)],
        cost_estimate=pl.CostEstimate(flops=0, bytes_accessed=10_000_000, transcendentals=0),
    )(blocks, neighbours, jnp.transpose(slope_weights, (1, 0, 2)))


def ranks(present):
    ids = jnp.arange(NB, dtype=jnp.int32)
    before = (ids[:, None] < ids[None, :])[None]
    return jnp.sum((present[:, :, None] & before).astype(jnp.int32), axis=1)


def blocks_of_slots(present, rank, slots):
    ids = jnp.arange(NB, dtype=jnp.int32)
    wanted = jnp.arange(slots, dtype=jnp.int32)
    match = present[:, :, None] & (rank[:, :, None] == wanted[None, None, :])
    return jnp.sum(jnp.where(match, ids[None, :, None], 0), axis=1)


def slopes_and_moments(window, words):
    low_block, mid_block, high_block = window
    east_code, north_code = unpack(words[0:K])
    east_weight = decode(east_code, WEIGHT_BOUND)
    north_weight = decode(north_code, WEIGHT_BOUND)
    first, second = unpack(words[K : K + 3])
    own = [decode(code, FIELD_BOUND) for code in unpack(mid_block)]
    east = [jnp.zeros_like(own[0]) for _ in own]
    north = [jnp.zeros_like(own[0]) for _ in own]
    shape = mid_block.shape
    for k in range(K):
        row = first[k : k + 1] if k < 3 else second[k - 3 : k - 2]
        place = jnp.broadcast_to(row, shape)
        lane = place & (BLK - 1)
        picked = [
            jnp.take_along_axis(part, lane, axis=1, mode="promise_in_bounds")
            for part in (low_block, mid_block, high_block)
        ]
        word = jnp.where(place < BLK, picked[0], jnp.where(place < 2 * BLK, picked[1], picked[2]))
        for side, code in enumerate(unpack(word)):
            difference = decode(code, FIELD_BOUND) - own[side]
            east[side] = east[side] + east_weight[k : k + 1] * difference
            north[side] = north[side] + north_weight[k : k + 1] * difference
    return [jnp.concatenate(part, axis=0).astype(jnp.bfloat16) for part in (own, east, north)]


def remap_kernel(parts, shares, *refs):
    me_ref, block_ref, slot_ref, dest_ref, order_ref, *refs = refs
    geometry_refs, refs = refs[:shares], refs[shares:]
    weights_ref, *refs = refs
    shards, refs = refs[: len(parts)], refs[len(parts) :]
    out_ref, top_ref, bottom_ref, field, even, odd, weights, total, field_sem, weight_sem = refs
    partitions, slots = block_ref.shape
    blocks = partitions * NB
    chunk = slot_ref.shape[0] // partitions
    share = slots // shares
    ahead = partitions // 4
    me, first_share = me_ref[0], me_ref[1]

    copies = []
    for (code, start, size), shard in zip(parts, shards):
        if code is None:
            target = field
        else:
            lanes = pl.ds(pl.multiple_of((me ^ code) * CELLS + start, BLK), size)
            target = field.at[:, lanes]
        copies.append(pltpu.make_async_copy(shard, target, field_sem))
    for copy in copies:
        copy.start()

    def fetch(q):
        for i in range(chunk):
            e = q * chunk + i
            pltpu.make_async_copy(weights_ref.at[order_ref[e]], weights.at[e], weight_sem.at[q]).start(priority=1)

    def arrived(q):
        piece = pl.ds(q * chunk, chunk)
        pltpu.make_async_copy(weights_ref.at[pl.ds(0, chunk)], weights.at[piece], weight_sem.at[q]).wait()

    def fetch_one(q, carry):
        fetch(q)
        return carry

    lax.fori_loop(0, ahead, fetch_one, 0)
    total[...] = jnp.zeros_like(total)
    for copy in copies:
        copy.wait()

    def slot_moments(q, j, moments):
        part = j // share
        s = (part ^ first_share) * share + j % share
        block = q * NB + block_ref[q, s]
        window = []
        for shift in (-1, 0, 1):
            near = lax.rem(block + (shift + blocks), blocks)
            window.append(field[:, pl.ds(pl.multiple_of(near * BLK, BLK), BLK)])
        row = j % share * ROWS
        words = geometry_refs[part][q, row : row + ROWS, :]
        for m, moment in enumerate(slopes_and_moments(window, words)):
            moments[s, :, m * BLK : (m + 1) * BLK] = moment

    def pair_product(q, i, moments):
        e = q * chunk + i
        p = order_ref[e]
        product = jnp.dot(moments[slot_ref[p]], weights[e], preferred_element_type=jnp.float32)
        dest = dest_ref[p]
        rows = pl.ds(dest >> 3, 16, stride=LAT_DEV)
        total[dest & 7, rows, :] = total[dest & 7, rows, :] + product

    def step(q, here, there):
        later = jnp.minimum(q + 1, partitions - 1)

        @pl.when(q + ahead < partitions)
        def _():
            fetch(q + ahead)

        arrived(q)
        each = max(1, chunk // slots)
        for j in range(slots):
            slot_moments(later, j, there)
            for i in range(j * each, (j + 1) * each):
                pair_product(q, i, here)

    for j in range(slots):
        slot_moments(0, j, even)

    def two(h, carry):
        step(2 * h, even, odd)
        step(2 * h + 1, odd, even)
        return carry

    lax.fori_loop(0, partitions // 2, two, 0)
    levels = out_ref.shape[0]
    for o in range(LONB):
        lanes = slice(o * BLK, (o + 1) * BLK)
        out_ref[:, :, lanes] = total[o].reshape(levels, LAT_DEV, BLK)
        top_ref[:, lanes] = total[o, pl.ds(0, levels, stride=LAT_DEV), :]
        bottom_ref[:, lanes] = total[o, pl.ds(LAT_DEV - 1, levels, stride=LAT_DEV), :]


def remap(me, blocks, slot, dest, order, geometry, weights, parts, shards, levels):
    partitions, slots = blocks.shape
    total = (LONB, levels * LAT_DEV, BLK)
    edge = jax.ShapeDtypeStruct((levels, LONB * BLK), jnp.float32)
    return pl.pallas_call(
        functools.partial(remap_kernel, parts, len(geometry)),
        in_specs=[SMEM] * 5 + [VMEM] * len(geometry) + [ANY] + [ANY] * len(shards),
        out_specs=(VMEM, VMEM, VMEM),
        out_shape=(jax.ShapeDtypeStruct((levels, LAT_DEV, LONB * BLK), jnp.float32), edge, edge),
        scratch_shapes=[
            pltpu.VMEM((levels // 2, partitions * CELLS), jnp.int32),
            pltpu.VMEM((slots, levels, 3 * BLK), jnp.bfloat16),
            pltpu.VMEM((slots, levels, 3 * BLK), jnp.bfloat16),
            pltpu.VMEM(weights.shape, jnp.bfloat16),
            pltpu.VMEM(total, jnp.float32),
            pltpu.SemaphoreType.DMA,
            pltpu.SemaphoreType.DMA((partitions,)),
        ],
        compiler_params=pltpu.CompilerParams(vmem_limit_bytes=56 * 1024 * 1024),
    )(me, blocks, slot, dest, order, *geometry, weights, *shards)


def swap(array, code):
    return lax.ppermute(array, "src", [(i, i ^ code) for i in range(lax.axis_size("src"))])


def tie(*arrays):
    return lax.optimization_barrier(arrays)


def local(source_field, neighbours, slope_weights, pair_block, pair_dest, remap_weights):
    levels, cell_count = source_field.shape
    own_index = lax.axis_index("src")
    partitions = lax.axis_size("src")
    pair_total = pair_block.shape[1]
    slots = max(1, pair_total // partitions // 2)
    ids = jnp.arange(NB, dtype=jnp.int32)

    packed = pack_field(source_field)

    own_names = own_index * NB + ids
    asked = jnp.any(pair_block[:, :, None] == own_names[None, None, :], axis=1)
    outgoing_blocks = blocks_of_slots(asked, ranks(asked), slots)
    group = lax.axis_index("groups")
    shares = 2 if lax.axis_size("groups") == 2 else 1
    share = slots // shares
    if shares == 2:
        outgoing_blocks = lax.dynamic_slice_in_dim(outgoing_blocks, group * share, share, 1)
    chosen = choose_geometry(outgoing_blocks, neighbours, slope_weights)
    geometry = [lax.all_to_all(chosen, "src", split_axis=0, concat_axis=0, tiled=True)]
    first = jnp.zeros((), jnp.int32)
    if shares == 2:
        geometry.append(lax.ppermute(geometry[0], "groups", [(0, 1), (1, 0)]))
        first = group

    row = lax.dynamic_index_in_dim(pair_block, own_index, 0, keepdims=False)
    names = jnp.arange(partitions * NB, dtype=jnp.int32)
    same = row[:, None] == names[None, :]
    needed = jnp.any(same, axis=0).reshape(partitions, NB)
    rank = ranks(needed)
    blocks = blocks_of_slots(needed, rank, slots)
    slot = jnp.sum(jnp.where(same, rank.reshape(1, -1), 0), axis=1)
    pair_ids = jnp.arange(pair_total, dtype=jnp.int32)
    key = row // NB * pair_total + pair_ids
    place = jnp.sum((key[:, None] < key[None, :]).astype(jnp.int32), axis=0)
    order = jnp.sum(jnp.where(place[:, None] == pair_ids[None, :], pair_ids[:, None], 0), axis=0)

    if partitions == 16:
        far, z, y = swap(packed, 8), swap(packed, 4), swap(packed, 2)
        far, order, _ = tie(far, order, chosen)
        far_z, far_y = swap(far, 4), swap(far, 2)
        far_z, far_y, y, order, slot, blocks = tie(far_z, far_y, y, order, slot, blocks)
        far_diagonal, diagonal = swap(far_z, 2), swap(y, 4)
        held = [
            (0, packed),
            (2, y),
            (4, z),
            (6, diagonal),
            (8, far),
            (12, far_z),
            (10, far_y),
            (14, far_diagonal),
        ]
        held = held + [(code ^ 1, swap(array, 1)) for code, array in held]
        parts = [(code, 0, array.shape[1]) for code, array in held]
        shards = [array for _, array in held]
    else:
        whole = lax.all_gather(packed, "src", axis=1, tiled=True)
        parts, shards = [(None, 0, whole.shape[1])], [whole]

    me = jnp.stack([own_index, first])
    remapped, top, bottom = remap(
        me, blocks, slot, pair_dest[0], order, geometry, remap_weights, parts, shards, levels
    )
    up = [(i, i + 1) for i in range(partitions - 1)]
    down = [(i + 1, i) for i in range(partitions - 1)]
    below = lax.ppermute(bottom, "src", up)
    above = lax.ppermute(top, "src", down)
    padded = jnp.concatenate([below[:, None], remapped, above[:, None]], axis=1)
    meridional = 0.5 * (padded[:, 2:] - padded[:, :-2])
    return remapped, meridional


def solution(mesh):
    return jax.shard_map(
        local,
        mesh=mesh,
        in_specs=(
            P("groups", "src"),
            P(None, "src"),
            P(None, None, "src"),
            P(),
            P("src", None),
            P("src", None, None),
        ),
        out_specs=(P("groups", "src", None), P("groups", "src", None)),
        check_vma=False,
    )
```

```python
import functools

import jax
import jax.numpy as jnp
from jax import lax
from jax.experimental import pallas as pl
from jax.experimental.pallas import tpu as pltpu
from jax.sharding import PartitionSpec as P

K = 6
BLK = 128
HALO = 128
NB = 64
LAT_DEV = 8
LONB = 8
CELLS = NB * BLK
PAIR_BITS = 16
PAIRS = 1 << PAIR_BITS
SLOT_BITS = 6
EARLY = (2, 3, 4, 5, 8, 9, 10, 12)
SLOTS = 1 << SLOT_BITS
ROWS = 9
CODE = 32767.0
FIELD_BOUND = 6.0
WEIGHT_BOUND = 2.0
VMEM = pl.BlockSpec(memory_space=pltpu.VMEM)
SMEM = pl.BlockSpec(memory_space=pltpu.SMEM)
ANY = pl.BlockSpec(memory_space=pl.ANY)


def encode(values, bound):
    scaled = jnp.abs(values) * (1.0 / bound)
    root = jnp.exp2(jnp.log2(jnp.maximum(scaled, 1e-30)) * 0.2)
    code = jnp.minimum(jnp.floor(root * CODE + 0.5), CODE)
    code = jnp.where(scaled > 1e-24, code, 0.0)
    return jnp.where(values < 0, -code, code).astype(jnp.int32)


def pack(high, low):
    return high * 65536 + (low + 32768)


def unpack(word):
    return word >> 16, (word & 65535) - 32768


def decode(code, bound):
    real = code.astype(jnp.float32)
    square = real * real
    return square * square * (real * (bound / CODE**5))


def pack_field_kernel(field_ref, out_ref):
    half = field_ref.shape[0] // 2
    step = 1024

    def piece(i, carry):
        lanes = pl.ds(pl.multiple_of(i * step, step), step)
        high = encode(field_ref[:half, lanes], FIELD_BOUND)
        low = encode(field_ref[half:, lanes], FIELD_BOUND)
        out_ref[:, lanes] = pack(high, low)
        return carry

    lax.fori_loop(0, field_ref.shape[1] // step, piece, 0)


def pack_field(field):
    levels, cells = field.shape
    return pl.pallas_call(
        pack_field_kernel,
        in_specs=[VMEM],
        out_specs=VMEM,
        out_shape=jax.ShapeDtypeStruct((levels // 2, cells), jnp.int32),
    )(field)


def geometry_kernel(first_ref, block_ref, neighbours_ref, weights_ref, out_ref, packed):
    tiles, slots = out_ref.shape[0], out_ref.shape[1] // ROWS
    first = first_ref[0]
    cells = neighbours_ref.shape[1]
    step = 1024

    def piece(i, carry):
        lanes = pl.ds(pl.multiple_of(i * step, step), step)
        column = lax.broadcasted_iota(jnp.int32, (1, step), 1) + i * step
        start = (column >> 7) << 7
        relative = neighbours_ref[:, lanes] - start
        east = encode(weights_ref[:, 0, lanes], WEIGHT_BOUND)
        north = encode(weights_ref[:, 1, lanes], WEIGHT_BOUND)
        packed[:K, lanes] = pack(east, north)
        packed[K:ROWS, lanes] = pack(relative[: K // 2], relative[K // 2 :])
        return carry

    lax.fori_loop(0, cells // step, piece, 0)

    def tile(t, carry):
        for s in range(slots):
            lanes = pl.ds(pl.multiple_of(block_ref[t, first + s] * BLK, BLK), BLK)
            out_ref[t, s * ROWS : (s + 1) * ROWS, :] = packed[:ROWS, lanes]
        return carry

    lax.fori_loop(0, tiles, tile, 0)


def choose_geometry(first, slots, blocks, neighbours, slope_weights):
    tiles = blocks.shape[0]
    return pl.pallas_call(
        geometry_kernel,
        in_specs=[SMEM, SMEM, VMEM, VMEM],
        out_specs=VMEM,
        out_shape=jax.ShapeDtypeStruct((tiles, slots * ROWS, BLK), jnp.int32),
        scratch_shapes=[pltpu.VMEM((16, neighbours.shape[1]), jnp.int32)],
        cost_estimate=pl.CostEstimate(flops=0, bytes_accessed=10_000_000, transcendentals=0),
    )(first, blocks, neighbours, jnp.transpose(slope_weights, (1, 0, 2)))


def ranks(present):
    ids = jnp.arange(NB, dtype=jnp.int32)
    before = (ids[:, None] < ids[None, :])[None]
    return jnp.sum((present[:, :, None] & before).astype(jnp.int32), axis=1)


def blocks_of_slots(present, rank, slots):
    ids = jnp.arange(NB, dtype=jnp.int32)
    wanted = jnp.arange(slots, dtype=jnp.int32)
    match = present[:, :, None] & (rank[:, :, None] == wanted[None, None, :])
    return jnp.sum(jnp.where(match, ids[None, :, None], 0), axis=1)


def slopes_and_moments(window, words):
    low_block, mid_block, high_block = window
    east_code, north_code = unpack(words[0:K])
    east_weight = decode(east_code, WEIGHT_BOUND)
    north_weight = decode(north_code, WEIGHT_BOUND)
    first, second = unpack(words[K : K + 3])
    own = [decode(code, FIELD_BOUND) for code in unpack(mid_block)]
    east = [jnp.zeros_like(own[0]) for _ in own]
    north = [jnp.zeros_like(own[0]) for _ in own]
    shape = mid_block.shape
    for k in range(K):
        row = first[k : k + 1] if k < 3 else second[k - 3 : k - 2]
        place = jnp.broadcast_to(row, shape)
        lane = place & (BLK - 1)
        picked = [
            jnp.take_along_axis(part, lane, axis=1, mode="promise_in_bounds")
            for part in (low_block, mid_block, high_block)
        ]
        word = jnp.where(place < BLK, picked[0], jnp.where(place < 2 * BLK, picked[1], picked[2]))
        for side, code in enumerate(unpack(word)):
            difference = decode(code, FIELD_BOUND) - own[side]
            east[side] = east[side] + east_weight[k : k + 1] * difference
            north[side] = north[side] + north_weight[k : k + 1] * difference
    return [jnp.concatenate(part, axis=0).astype(jnp.bfloat16) for part in (own, east, north)]


def remap_kernel(parts, shares, *refs):
    me_ref, block_ref, table_ref, *refs = refs
    geometry_refs, refs = refs[:shares], refs[shares:]
    weights_ref, *refs = refs
    shards, refs = refs[: len(parts)], refs[len(parts) :]
    out_ref, near_ref, next_ref, field, even, odd, weights, total, field_sem, weight_sem = refs
    partitions, slots = block_ref.shape
    blocks = partitions * NB
    chunk = table_ref.shape[0] // partitions
    share = slots // shares
    ahead = partitions // 4
    me, first_share = me_ref[0], me_ref[1]

    copies = []
    for (code, start, size), shard in zip(parts, shards):
        if code is None:
            target = field
        else:
            lanes = pl.ds(pl.multiple_of((me ^ code) * CELLS + start, BLK), size)
            target = field.at[:, lanes]
        copies.append(pltpu.make_async_copy(shard, target, field_sem))
    for copy in copies:
        copy.start()

    def fetch(q):
        for i in range(chunk):
            e = q * chunk + i
            pair = table_ref[e] & (PAIRS - 1)
            pltpu.make_async_copy(weights_ref.at[pair], weights.at[e], weight_sem.at[q]).start(priority=1)

    def arrived(q):
        piece = pl.ds(q * chunk, chunk)
        pltpu.make_async_copy(weights_ref.at[pl.ds(0, chunk)], weights.at[piece], weight_sem.at[q]).wait()

    def fetch_one(q, carry):
        fetch(q)
        return carry

    lax.fori_loop(0, ahead, fetch_one, 0)
    total[...] = jnp.zeros_like(total)
    for copy in copies:
        copy.wait()

    def slot_moments(q, j, moments):
        part = j // share
        s = (part ^ first_share) * share + j % share
        block = q * NB + block_ref[q, s]
        window = []
        for shift in (-1, 0, 1):
            near = lax.rem(block + (shift + blocks), blocks)
            window.append(field[:, pl.ds(pl.multiple_of(near * BLK, BLK), BLK)])
        row = j % share * ROWS
        words = geometry_refs[part][q, row : row + ROWS, :]
        for m, moment in enumerate(slopes_and_moments(window, words)):
            moments[s, :, m * BLK : (m + 1) * BLK] = moment

    def pair_product(q, i, moments):
        e = q * chunk + i
        word = table_ref[e] >> PAIR_BITS
        dest = word >> SLOT_BITS
        product = jnp.dot(moments[word & (SLOTS - 1)], weights[e], preferred_element_type=jnp.float32)
        rows = pl.ds(dest >> 3, 16, stride=LAT_DEV)
        total[dest & 7, rows, :] = total[dest & 7, rows, :] + product

    def step(q, here, there):
        later = jnp.minimum(q + 1, partitions - 1)

        @pl.when(q + ahead < partitions)
        def _():
            fetch(q + ahead)

        arrived(q)
        each = max(1, chunk // slots)
        for j in range(slots):
            slot_moments(later, j, there)
            for i in range(j * each, (j + 1) * each):
                pair_product(q, i, here)

    for j in range(slots):
        slot_moments(0, j, even)

    def two(h, carry):
        step(2 * h, even, odd)
        step(2 * h + 1, odd, even)
        return carry

    lax.fori_loop(0, partitions // 2, two, 0)
    levels = out_ref.shape[0]
    for o in range(LONB):
        lanes = slice(o * BLK, (o + 1) * BLK)
        out_ref[:, :, lanes] = total[o].reshape(levels, LAT_DEV, BLK)
        top = total[o, pl.ds(0, levels, stride=LAT_DEV), :]
        bottom = total[o, pl.ds(LAT_DEV - 1, levels, stride=LAT_DEV), :]
        near_ref[:, lanes] = jnp.where(me & 1 == 0, bottom, top)
        next_ref[:, lanes] = jnp.where(me & 1 == 0, top, bottom)


def remap(me, blocks, table, geometry, weights, parts, shards, levels):
    partitions, slots = blocks.shape
    total = (LONB, levels * LAT_DEV, BLK)
    edge = jax.ShapeDtypeStruct((levels, LONB * BLK), jnp.float32)
    return pl.pallas_call(
        functools.partial(remap_kernel, parts, len(geometry)),
        in_specs=[SMEM] * 3 + [VMEM] * len(geometry) + [ANY] + [ANY] * len(shards),
        out_specs=(VMEM, VMEM, VMEM),
        out_shape=(jax.ShapeDtypeStruct((levels, LAT_DEV, LONB * BLK), jnp.float32), edge, edge),
        scratch_shapes=[
            pltpu.VMEM((levels // 2, partitions * CELLS), jnp.int32),
            pltpu.VMEM((slots, levels, 3 * BLK), jnp.bfloat16),
            pltpu.VMEM((slots, levels, 3 * BLK), jnp.bfloat16),
            pltpu.VMEM(weights.shape, jnp.bfloat16),
            pltpu.VMEM(total, jnp.float32),
            pltpu.SemaphoreType.DMA,
            pltpu.SemaphoreType.DMA((partitions,)),
        ],
        compiler_params=pltpu.CompilerParams(vmem_limit_bytes=44 * 1024 * 1024),
    )(me, blocks, table, *geometry, weights, *shards)


def swap(array, code):
    return lax.ppermute(array, "src", [(i, i ^ code) for i in range(lax.axis_size("src"))])


def tie(*arrays):
    return lax.optimization_barrier(arrays)


def local(source_field, neighbours, slope_weights, pair_block, pair_dest, remap_weights):
    levels, cell_count = source_field.shape
    own_index = lax.axis_index("src")
    partitions = lax.axis_size("src")
    pair_total = pair_block.shape[1]
    slots = max(1, pair_total // partitions // 2)
    ids = jnp.arange(NB, dtype=jnp.int32)

    packed = pack_field(source_field)

    own_names = own_index * NB + ids
    asked = jnp.any(pair_block[:, :, None] == own_names[None, None, :], axis=1)
    outgoing_blocks = blocks_of_slots(asked, ranks(asked), slots)
    group = lax.axis_index("groups")
    shares = 2 if lax.axis_size("groups") == 2 else 1
    share = slots // shares
    start = (group * share if shares == 2 else jnp.zeros((), jnp.int32)).reshape(1)
    chosen = choose_geometry(start, share, outgoing_blocks, neighbours, slope_weights)
    geometry = [lax.all_to_all(chosen, "src", split_axis=0, concat_axis=0, tiled=True)]
    first = jnp.zeros((), jnp.int32)
    if shares == 2:
        geometry.append(lax.ppermute(geometry[0], "groups", [(0, 1), (1, 0)]))
        first = group

    pair_block, _ = tie(pair_block, chosen)
    row = lax.dynamic_index_in_dim(pair_block, own_index, 0, keepdims=False)
    names = jnp.arange(partitions * NB, dtype=jnp.int32)
    same = row[:, None] == names[None, :]
    needed = jnp.any(same, axis=0).reshape(partitions, NB)
    rank = ranks(needed)
    blocks = blocks_of_slots(needed, rank, slots)
    slot = jnp.sum(jnp.where(same, rank.reshape(1, -1), 0), axis=1)
    word = (pair_dest[0] * SLOTS + slot) * PAIRS + jnp.arange(pair_total, dtype=jnp.int32)
    pair_ids = jnp.arange(pair_total, dtype=jnp.int32)
    key = row // NB * pair_total + pair_ids
    place = jnp.sum((key[:, None] < key[None, :]).astype(jnp.int32), axis=0)
    table = jnp.sum(jnp.where(place[:, None] == pair_ids[None, :], word[:, None], 0), axis=0)

    me = jnp.stack([own_index, first])
    if partitions == 16:
        far, z, y = swap(packed, 8), swap(packed, 4), swap(packed, 2)
        far, _ = tie(far, chosen)
        diagonal = swap(y, 4)
        far_z, far_y = swap(far, 4), swap(far, 2)
        far_z, far_y, table, blocks, me = tie(far_z, far_y, table, blocks, me)
        far_diagonal = swap(far_z, 2)
        held = [
            (0, packed),
            (2, y),
            (4, z),
            (6, diagonal),
            (8, far),
            (12, far_z),
            (10, far_y),
            (14, far_diagonal),
        ]
        held = held + [(code ^ 1, swap(array, 1)) for code, array in held]
        parts = [(code, 0, array.shape[1]) for code, array in held]
        shards = [pltpu.with_memory_space_constraint(array, pltpu.VMEM) if code in EARLY else array for code, array in held]
    else:
        whole = lax.all_gather(packed, "src", axis=1, tiled=True)
        parts, shards = [(None, 0, whole.shape[1])], [whole]

    remapped, near, beyond = remap(
        me, blocks, table, geometry, remap_weights, parts, shards, levels
    )
    steps = [(i, i + 1) for i in range(1, partitions - 1, 2)]
    beyond = lax.ppermute(beyond, "src", steps + [(j, i) for i, j in steps])
    near = swap(near, 1)
    even = own_index % 2 == 0
    below = jnp.where(even, beyond, near)
    above = jnp.where(even, near, beyond)
    padded = jnp.concatenate([below[:, None], remapped, above[:, None]], axis=1)
    meridional = 0.5 * (padded[:, 2:] - padded[:, :-2])
    return remapped, meridional


def solution(mesh):
    return jax.shard_map(
        local,
        mesh=mesh,
        in_specs=(
            P("groups", "src"),
            P(None, "src"),
            P(None, None, "src"),
            P(),
            P("src", None),
            P("src", None, None),
        ),
        out_specs=(P("groups", "src", None), P("groups", "src", None)),
        check_vma=False,
    )
```

```python
import functools

import jax
import jax.numpy as jnp
from jax import lax
from jax.experimental import pallas as pl
from jax.experimental.pallas import tpu as pltpu
from jax.sharding import PartitionSpec as P

K = 6
BLK = 128
HALO = 128
NB = 64
LAT_DEV = 8
LONB = 8
CELLS = NB * BLK
PAIR_BITS = 16
PAIRS = 1 << PAIR_BITS
SLOT_BITS = 6
EARLY = (2, 3, 4, 5, 8, 9, 10, 12)
SLOTS = 1 << SLOT_BITS
ROWS = 9
CODE = 32767.0
FIELD_BOUND = 6.0
WEIGHT_BOUND = 2.0
VMEM = pl.BlockSpec(memory_space=pltpu.VMEM)
SMEM = pl.BlockSpec(memory_space=pltpu.SMEM)
ANY = pl.BlockSpec(memory_space=pl.ANY)


def encode(values, bound):
    scaled = jnp.abs(values) * (1.0 / bound)
    root = jnp.exp2(jnp.log2(jnp.maximum(scaled, 1e-30)) * 0.2)
    code = jnp.minimum(jnp.floor(root * CODE + 0.5), CODE)
    code = jnp.where(scaled > 1e-24, code, 0.0)
    return jnp.where(values < 0, -code, code).astype(jnp.int32)


def pack(high, low):
    return high * 65536 + (low + 32768)


def unpack(word):
    return word >> 16, (word & 65535) - 32768


def decode(code, bound):
    real = code.astype(jnp.float32)
    square = real * real
    return square * square * (real * (bound / CODE**5))


def pack_field_kernel(field_ref, out_ref):
    half = field_ref.shape[0] // 2
    step = 1024

    def piece(i, carry):
        lanes = pl.ds(pl.multiple_of(i * step, step), step)
        high = encode(field_ref[:half, lanes], FIELD_BOUND)
        low = encode(field_ref[half:, lanes], FIELD_BOUND)
        out_ref[:, lanes] = pack(high, low)
        return carry

    lax.fori_loop(0, field_ref.shape[1] // step, piece, 0)


def pack_field(field):
    levels, cells = field.shape
    return pl.pallas_call(
        pack_field_kernel,
        in_specs=[VMEM],
        out_specs=VMEM,
        out_shape=jax.ShapeDtypeStruct((levels // 2, cells), jnp.int32),
    )(field)


def geometry_kernel(first_ref, block_ref, neighbours_ref, weights_ref, out_ref, packed):
    tiles, slots = out_ref.shape[0], out_ref.shape[1] // ROWS
    first = first_ref[0]
    cells = neighbours_ref.shape[1]
    step = 1024

    def piece(i, carry):
        lanes = pl.ds(pl.multiple_of(i * step, step), step)
        column = lax.broadcasted_iota(jnp.int32, (1, step), 1) + i * step
        start = (column >> 7) << 7
        relative = neighbours_ref[:, lanes] - start
        east = encode(weights_ref[:, 0, lanes], WEIGHT_BOUND)
        north = encode(weights_ref[:, 1, lanes], WEIGHT_BOUND)
        packed[:K, lanes] = pack(east, north)
        packed[K:ROWS, lanes] = pack(relative[: K // 2], relative[K // 2 :])
        return carry

    lax.fori_loop(0, cells // step, piece, 0)

    def tile(t, carry):
        for s in range(slots):
            lanes = pl.ds(pl.multiple_of(block_ref[t, first + s] * BLK, BLK), BLK)
            out_ref[t, s * ROWS : (s + 1) * ROWS, :] = packed[:ROWS, lanes]
        return carry

    lax.fori_loop(0, tiles, tile, 0)


def choose_geometry(first, slots, blocks, neighbours, slope_weights):
    tiles = blocks.shape[0]
    return pl.pallas_call(
        geometry_kernel,
        in_specs=[SMEM, SMEM, VMEM, VMEM],
        out_specs=VMEM,
        out_shape=jax.ShapeDtypeStruct((tiles, slots * ROWS, BLK), jnp.int32),
        scratch_shapes=[pltpu.VMEM((16, neighbours.shape[1]), jnp.int32)],
        cost_estimate=pl.CostEstimate(flops=0, bytes_accessed=10_000_000, transcendentals=0),
    )(first, blocks, neighbours, jnp.transpose(slope_weights, (1, 0, 2)))


def ranks(present):
    ids = jnp.arange(NB, dtype=jnp.int32)
    before = (ids[:, None] < ids[None, :])[None]
    return jnp.sum((present[:, :, None] & before).astype(jnp.int32), axis=1)


def blocks_of_slots(present, rank, slots):
    ids = jnp.arange(NB, dtype=jnp.int32)
    wanted = jnp.arange(slots, dtype=jnp.int32)
    match = present[:, :, None] & (rank[:, :, None] == wanted[None, None, :])
    return jnp.sum(jnp.where(match, ids[None, :, None], 0), axis=1)


def slopes_and_moments(window, words):
    low_block, mid_block, high_block = window
    east_code, north_code = unpack(words[0:K])
    east_weight = decode(east_code, WEIGHT_BOUND)
    north_weight = decode(north_code, WEIGHT_BOUND)
    first, second = unpack(words[K : K + 3])
    own = [decode(code, FIELD_BOUND) for code in unpack(mid_block)]
    east = [jnp.zeros_like(own[0]) for _ in own]
    north = [jnp.zeros_like(own[0]) for _ in own]
    shape = mid_block.shape
    for k in range(K):
        row = first[k : k + 1] if k < 3 else second[k - 3 : k - 2]
        place = jnp.broadcast_to(row, shape)
        lane = place & (BLK - 1)
        picked = [
            jnp.take_along_axis(part, lane, axis=1, mode="promise_in_bounds")
            for part in (low_block, mid_block, high_block)
        ]
        word = jnp.where(place < BLK, picked[0], jnp.where(place < 2 * BLK, picked[1], picked[2]))
        for side, code in enumerate(unpack(word)):
            difference = decode(code, FIELD_BOUND) - own[side]
            east[side] = east[side] + east_weight[k : k + 1] * difference
            north[side] = north[side] + north_weight[k : k + 1] * difference
    return [jnp.concatenate(part, axis=0).astype(jnp.bfloat16) for part in (own, east, north)]


def remap_kernel(parts, shares, *refs):
    me_ref, block_ref, table_ref, *refs = refs
    geometry_refs, refs = refs[:shares], refs[shares:]
    early_weights, weights_ref, *refs = refs
    shards, refs = refs[: len(parts)], refs[len(parts) :]
    out_ref, near_ref, next_ref, field, even, odd, weights, total, field_sem, weight_sem = refs
    partitions, slots = block_ref.shape
    blocks = partitions * NB
    chunk = table_ref.shape[0] // partitions
    share = slots // shares
    ahead = partitions // 4
    kept = early_weights.shape[0] // chunk
    me, first_share = me_ref[0], me_ref[1]

    copies = []
    for (code, start, size), shard in zip(parts, shards):
        if code is None:
            target = field
        else:
            lanes = pl.ds(pl.multiple_of((me ^ code) * CELLS + start, BLK), size)
            target = field.at[:, lanes]
        copies.append(pltpu.make_async_copy(shard, target, field_sem))
    for copy in copies:
        copy.start()

    def fetch(q):
        for i in range(chunk):
            e = q * chunk + i
            pair = table_ref[e] & (PAIRS - 1)
            target = weights.at[e - kept * chunk]
            pltpu.make_async_copy(weights_ref.at[pair], target, weight_sem.at[q]).start(priority=1)

    def arrived(q):
        piece = pl.ds((q - kept) * chunk, chunk)
        pltpu.make_async_copy(weights_ref.at[pl.ds(0, chunk)], weights.at[piece], weight_sem.at[q]).wait()

    def fetch_one(q, carry):
        fetch(q)
        return carry

    lax.fori_loop(kept, kept + ahead, fetch_one, 0)
    total[...] = jnp.zeros_like(total)
    for copy in copies:
        copy.wait()

    def slot_moments(q, j, moments):
        part = j // share
        s = (part ^ first_share) * share + j % share
        block = q * NB + block_ref[q, s]
        window = []
        for shift in (-1, 0, 1):
            near = lax.rem(block + (shift + blocks), blocks)
            window.append(field[:, pl.ds(pl.multiple_of(near * BLK, BLK), BLK)])
        row = j % share * ROWS
        words = geometry_refs[part][q, row : row + ROWS, :]
        for m, moment in enumerate(slopes_and_moments(window, words)):
            moments[s, :, m * BLK : (m + 1) * BLK] = moment

    def pair_product(q, i, moments, source, first):
        e = q * chunk + i
        word = table_ref[e] >> PAIR_BITS
        dest = word >> SLOT_BITS
        product = jnp.dot(moments[word & (SLOTS - 1)], source[e - first], preferred_element_type=jnp.float32)
        rows = pl.ds(dest >> 3, 16, stride=LAT_DEV)
        total[dest & 7, rows, :] = total[dest & 7, rows, :] + product

    def step(q, here, there, streamed):
        later = jnp.minimum(q + 1, partitions - 1)

        if streamed:

            @pl.when(q + ahead < partitions)
            def _():
                fetch(q + ahead)

            arrived(q)
        each = max(1, chunk // slots)
        for j in range(slots):
            slot_moments(later, j, there)
            for i in range(j * each, (j + 1) * each):
                pair_product(q, i, here, *((weights, kept * chunk) if streamed else (early_weights, 0)))

    for j in range(slots):
        slot_moments(0, j, even)

    def two(streamed, h, carry):
        step(2 * h, even, odd, streamed)
        step(2 * h + 1, odd, even, streamed)
        return carry

    lax.fori_loop(0, kept // 2, functools.partial(two, False), 0)
    lax.fori_loop(kept // 2, partitions // 2, functools.partial(two, True), 0)
    levels = out_ref.shape[0]
    for o in range(LONB):
        lanes = slice(o * BLK, (o + 1) * BLK)
        out_ref[:, :, lanes] = total[o].reshape(levels, LAT_DEV, BLK)
        top = total[o, pl.ds(0, levels, stride=LAT_DEV), :]
        bottom = total[o, pl.ds(LAT_DEV - 1, levels, stride=LAT_DEV), :]
        near_ref[:, lanes] = jnp.where(me & 1 == 0, bottom, top)
        next_ref[:, lanes] = jnp.where(me & 1 == 0, top, bottom)


def remap(me, blocks, table, geometry, early, weights, parts, shards, levels):
    partitions, slots = blocks.shape
    total = (LONB, levels * LAT_DEV, BLK)
    edge = jax.ShapeDtypeStruct((levels, LONB * BLK), jnp.float32)
    return pl.pallas_call(
        functools.partial(remap_kernel, parts, len(geometry)),
        in_specs=[SMEM] * 3 + [VMEM] * len(geometry) + [VMEM, ANY] + [ANY] * len(shards),
        out_specs=(VMEM, VMEM, VMEM),
        out_shape=(jax.ShapeDtypeStruct((levels, LAT_DEV, LONB * BLK), jnp.float32), edge, edge),
        scratch_shapes=[
            pltpu.VMEM((levels // 2, partitions * CELLS), jnp.int32),
            pltpu.VMEM((slots, levels, 3 * BLK), jnp.bfloat16),
            pltpu.VMEM((slots, levels, 3 * BLK), jnp.bfloat16),
            pltpu.VMEM((weights.shape[0] - early.shape[0],) + weights.shape[1:], jnp.bfloat16),
            pltpu.VMEM(total, jnp.float32),
            pltpu.SemaphoreType.DMA,
            pltpu.SemaphoreType.DMA((partitions,)),
        ],
        compiler_params=pltpu.CompilerParams(vmem_limit_bytes=38 * 1024 * 1024),
    )(me, blocks, table, *geometry, early, weights, *shards)


def preload_kernel(chunk, table_ref, weights_ref, after_ref, array_ref, out_ref, array_out, sem, array_sem):
    count = out_ref.shape[0]
    copy = pltpu.make_async_copy(array_ref, array_out, array_sem)
    copy.start()

    def fetch(c, carry):
        for i in range(chunk):
            e = c * chunk + i
            pair = table_ref[e] & (PAIRS - 1)
            pltpu.make_async_copy(weights_ref.at[pair], out_ref.at[e], sem).start()
        return carry

    lax.fori_loop(0, count // chunk, fetch, 0)
    copy.wait()
    pltpu.make_async_copy(weights_ref.at[pl.ds(0, count)], out_ref, sem).wait()


def preload(count, table, weights, after, array):
    kept, array = pl.pallas_call(
        functools.partial(preload_kernel, 16),
        in_specs=[SMEM, ANY, ANY, ANY],
        out_specs=(VMEM, ANY),
        out_shape=(
            pltpu.VMEM((count,) + weights.shape[1:], weights.dtype),
            jax.ShapeDtypeStruct(array.shape, array.dtype),
        ),
        scratch_shapes=[pltpu.SemaphoreType.DMA, pltpu.SemaphoreType.DMA],
        compiler_params=pltpu.CompilerParams(vmem_limit_bytes=40 * 1024 * 1024),
    )(table, weights, after, array)
    return pltpu.with_memory_space_constraint(kept, pltpu.VMEM), array


def swap(array, code):
    return lax.ppermute(array, "src", [(i, i ^ code) for i in range(lax.axis_size("src"))])


def tie(*arrays):
    return lax.optimization_barrier(arrays)


def local(source_field, neighbours, slope_weights, pair_block, pair_dest, remap_weights):
    levels, cell_count = source_field.shape
    own_index = lax.axis_index("src")
    partitions = lax.axis_size("src")
    pair_total = pair_block.shape[1]
    slots = max(1, pair_total // partitions // 2)
    ids = jnp.arange(NB, dtype=jnp.int32)

    packed = pack_field(source_field)

    own_names = own_index * NB + ids
    asked = jnp.any(pair_block[:, :, None] == own_names[None, None, :], axis=1)
    outgoing_blocks = blocks_of_slots(asked, ranks(asked), slots)
    group = lax.axis_index("groups")
    shares = 2 if lax.axis_size("groups") == 2 else 1
    share = slots // shares
    start = (group * share if shares == 2 else jnp.zeros((), jnp.int32)).reshape(1)
    chosen = choose_geometry(start, share, outgoing_blocks, neighbours, slope_weights)
    geometry = [lax.all_to_all(chosen, "src", split_axis=0, concat_axis=0, tiled=True)]
    first = jnp.zeros((), jnp.int32)
    if shares == 2:
        geometry.append(lax.ppermute(geometry[0], "groups", [(0, 1), (1, 0)]))
        first = group

    pair_block, _ = tie(pair_block, chosen)
    row = lax.dynamic_index_in_dim(pair_block, own_index, 0, keepdims=False)
    names = jnp.arange(partitions * NB, dtype=jnp.int32)
    same = row[:, None] == names[None, :]
    needed = jnp.any(same, axis=0).reshape(partitions, NB)
    rank = ranks(needed)
    blocks = blocks_of_slots(needed, rank, slots)
    slot = jnp.sum(jnp.where(same, rank.reshape(1, -1), 0), axis=1)
    word = (pair_dest[0] * SLOTS + slot) * PAIRS + jnp.arange(pair_total, dtype=jnp.int32)
    pair_ids = jnp.arange(pair_total, dtype=jnp.int32)
    key = row // NB * pair_total + pair_ids
    place = jnp.sum((key[:, None] < key[None, :]).astype(jnp.int32), axis=0)
    table = jnp.sum(jnp.where(place[:, None] == pair_ids[None, :], word[:, None], 0), axis=0)

    me = jnp.stack([own_index, first])
    remap_weights = pltpu.with_memory_space_constraint(remap_weights, pltpu.HBM)
    if partitions == 16:
        far, z, y = swap(packed, 8), swap(packed, 4), swap(packed, 2)
        far, _ = tie(far, chosen)
        diagonal = swap(y, 4)
        far_z, far_y = swap(far, 4), swap(far, 2)
        far_z, far_y, table, blocks, me = tie(far_z, far_y, table, blocks, me)
        far_diagonal = swap(far_z, 2)
        early_weights, again = preload(pair_total // 4, table, remap_weights, far_z, far_z)
        held = [
            (0, packed),
            (2, y),
            (4, z),
            (6, diagonal),
            (8, far),
            (12, far_z),
            (10, far_y),
            (14, far_diagonal),
        ]
        held = held + [(code ^ 1, swap(again if code == 12 else array, 1)) for code, array in held]
        parts = [(code, 0, array.shape[1]) for code, array in held]
        shards = [pltpu.with_memory_space_constraint(array, pltpu.VMEM) if code in EARLY else array for code, array in held]
    else:
        early_weights, packed = preload(pair_total // 4, table, remap_weights, packed, packed)
        whole = lax.all_gather(packed, "src", axis=1, tiled=True)
        parts, shards = [(None, 0, whole.shape[1])], [whole]

    remapped, near, beyond = remap(
        me, blocks, table, geometry, early_weights, remap_weights, parts, shards, levels
    )
    steps = [(i, i + 1) for i in range(1, partitions - 1, 2)]
    beyond = lax.ppermute(beyond, "src", steps + [(j, i) for i, j in steps])
    near = swap(near, 1)
    even = own_index % 2 == 0
    below = jnp.where(even, beyond, near)
    above = jnp.where(even, near, beyond)
    padded = jnp.concatenate([below[:, None], remapped, above[:, None]], axis=1)
    meridional = 0.5 * (padded[:, 2:] - padded[:, :-2])
    return remapped, meridional


def solution(mesh):
    return jax.shard_map(
        local,
        mesh=mesh,
        in_specs=(
            P("groups", "src"),
            P(None, "src"),
            P(None, None, "src"),
            P(),
            P("src", None),
            P("src", None, None),
        ),
        out_specs=(P("groups", "src", None), P("groups", "src", None)),
        check_vma=False,
    )
```
